256 devices in a mesh: gx: 8 (over x, core), gy: 32 (over z, y).
Axes of the slice: x: 4, y: 4, z: 8, core: 2. Of those that a mesh axis runs over, the one named last changes fastest.
Arguments:
- leaf_weights: bfloat16 [256, 343, 512], P(('gx', 'gy')), may hold values from -6 to 6
- compress: bfloat16 [64, 343], replicated, may hold values from -0.3125 to 0.3125
- expand: bfloat16 [343, 64], replicated, may hold values from -0.75 to 0.75
- transfer: bfloat16 [316, 64, 64], replicated, may hold values from -0.0625 to 0.0625
- shifts: bfloat16 [8, 343, 343], replicated, may hold values from -0.109375 to 0.109375
- boundary: int32 [256, 8, 256], P(('gx', 'gy')), may hold values from 0 to 511, as said below
- sources: int32 [256, 316, 512], P(('gx', 'gy')), may hold values from 0 to 2560, as said below
- coarse_sources: int32 [256, 316, 64], P(('gx', 'gy')), may hold values from 0 to 64, as said below
Outputs:
- leaf_locals: float32 [256, 343, 512], P(('gx', 'gy'))
- top_weights: float32 [256, 343], P(('gx', 'gy'))
The draws below stay inside these ranges and needn't reach their ends.
Inputs may be any that keep to these rules, and one draw needn't show every extreme that they name: The 256 entries of each row boundary[d, s] are distinct leaf cells of device d. `sources`: the value 2560 marks an offset without a source cell. `coarse_sources`: the value 64 marks an offset without a source cell.
All inputs are finite; a program needn't handle non-finite values.
Results may differ from the reference program's by a relative error of at most 0.006.
Values may be sent and summed in bfloat16 or wider, within the bound.
A program may use at most 128 MiB of HBM per device.

```python
import jax
import jax.numpy as jnp
from jax import lax

Q = 343
R = 64
NT = 316
C = 512
B = 256
SECTIONS = 8
DEVICES = 256


def draw_boundary(key, part):
    key = jax.random.fold_in(key, 11)
    row_keys = jax.random.split(key, DEVICES * SECTIONS)

    def one_row(row_key):
        return jax.random.permutation(row_key, C)[:B]
    rows = jax.vmap(one_row)(row_keys)
    return rows.reshape(DEVICES, SECTIONS, B).astype(jnp.int32)


def offset_lists(key, limit, targets):
    choose_key, present_key = jax.random.split(key)
    chosen_cells = jax.random.randint(choose_key, (DEVICES, NT, targets), 0, limit)
    present = jax.random.randint(present_key, (DEVICES, NT, targets), 0, 5) < 3
    return jnp.where(present, chosen_cells, limit).astype(jnp.int32)


def draw_sources(key, part):
    key = jax.random.fold_in(key, 23)
    return offset_lists(key, C + SECTIONS * B, C)


def draw_coarse_sources(key, part):
    key = jax.random.fold_in(key, 37)
    return offset_lists(key, C // 8, C // 8)


def block_scale(rng, dims, pieces, low, largest):
    factor_of = 1.0
    for axis_at, parts in pieces:
        heights = jax.random.uniform(jax.random.fold_in(jax.random.fold_in(rng, 6), axis_at), (parts,), jnp.float32, low / len(pieces), largest / len(pieces))
        factor_of = factor_of * jnp.repeat(jnp.exp(heights), dims[axis_at] // parts).reshape((-1,) + (1,) * (len(dims) - 1 - axis_at))
    return factor_of


def noise(stream_key, shape, deviation, most, pieces=(), kind=jnp.bfloat16):
    gain = block_scale(stream_key, shape, pieces, -0.22, 0.18) if pieces else 1.0
    values = jax.random.normal(stream_key, shape, jnp.float32) * deviation * gain
    return jnp.minimum(jnp.maximum(values, -most), most).astype(kind)


def setup_inputs(seed: int = 0) -> dict:
    key_of = jax.random.split(jax.random.key(seed), 9)
    leaf_weights = noise(key_of[0], (DEVICES, Q, C), 1.0, 6.0, ((0, 256),))
    compress = noise(key_of[1], (R, Q), Q ** -0.5, 0.3125)
    expand = noise(key_of[2], (Q, R), R ** -0.5, 0.75)
    transfer = noise(key_of[3], (NT, R, R), (R * NT // 2) ** -0.5, 0.0625)
    shifts = noise(key_of[4], (8, Q, Q), (8 * Q) ** -0.5, 0.109375)
    boundary = draw_boundary(jax.random.fold_in(key_of[8], 71), 0)
    sources = draw_sources(jax.random.fold_in(key_of[8], 71), 0)
    coarse_sources = draw_coarse_sources(jax.random.fold_in(key_of[8], 71), 0)
    return dict(leaf_weights=leaf_weights, compress=compress, expand=expand, transfer=transfer, shifts=shifts, boundary=boundary, sources=sources, coarse_sources=coarse_sources)


def upward(shifts, weights):
    children = weights.astype(jnp.float32).reshape(weights.shape[0], -1, 8)
    return jnp.einsum("kpq,qik->pi", shifts.astype(jnp.float32), children)


def translate(transfer, table, lists):
    gathered = jnp.take(table, lists, axis=1, mode="fill", fill_value=0)
    return jnp.einsum("jab,bjt->at", transfer.astype(jnp.float32), gathered.astype(jnp.float32))


def reference(leaf_weights, compress, expand, transfer, shifts, boundary, sources, coarse_sources):
    device_count = leaf_weights.shape[0]
    section_count = boundary.shape[1]
    packed = jnp.einsum("rq,dqc->drc", compress.astype(jnp.float32), leaf_weights.astype(jnp.float32)).astype(jnp.bfloat16)
    positions = jnp.arange(device_count, dtype=jnp.int32)
    columns = [packed]
    for section_index in range(section_count):
        partner = jnp.bitwise_xor(positions, 1 << section_index)
        chosen = boundary[partner, section_index]
        others = packed[partner]
        chosen = jnp.broadcast_to(chosen[:, None, :], (device_count, others.shape[1], chosen.shape[1]))
        columns.append(jnp.take_along_axis(others, chosen, axis=2))
    table = jnp.concatenate(columns, axis=2)

    def device_pass(operands):
        leaf_cells, device_table, leaf_lists, parent_lists = operands
        far_leaf = translate(transfer, device_table, leaf_lists).astype(jnp.bfloat16)
        current = leaf_cells
        levels = []
        while current.shape[1] > 1:
            current = upward(shifts, current).astype(jnp.bfloat16)
            levels.append(current)
        parents = levels[0]
        packed_parents = jnp.dot(compress, parents, preferred_element_type=jnp.float32).astype(jnp.bfloat16)
        far_parent = (0.5 * translate(transfer, packed_parents, parent_lists)).astype(jnp.bfloat16)
        local_parent = jnp.dot(expand, far_parent, preferred_element_type=jnp.float32).astype(jnp.bfloat16)
        downward = jnp.einsum("kpq,pi->qik", shifts.astype(jnp.float32), local_parent.astype(jnp.float32))
        downward = downward.reshape(shifts.shape[1], -1)
        leaf_locals = jnp.dot(expand, far_leaf, preferred_element_type=jnp.float32) + downward
        return leaf_locals, levels[-1][:, 0]

    leaf_locals, apex = lax.map(device_pass, (leaf_weights, table, sources, coarse_sources))
    octant = positions % 8
    octant_terms = jnp.einsum("dpq,dq->dp", shifts.astype(jnp.float32)[octant], apex.astype(jnp.float32))
    grouped = jnp.sum(octant_terms.reshape(-1, 8, octant_terms.shape[1]), axis=1)
    top_weights = jnp.repeat(grouped, 8, axis=0)
    return leaf_locals, top_weights
```

```python
import jax
import jax.numpy as jnp
from jax import lax
from jax.experimental import pallas as pl
from jax.experimental.pallas import tpu as pltpu
from jax.sharding import PartitionSpec as P

F32, BF16, F8 = jnp.float32, jnp.bfloat16, jnp.float8_e4m3fn
MESH = pl.DeviceIdType.MESH
VMEM = pl.BlockSpec(memory_space=pltpu.VMEM)
OFFSETS, CELLS, TABLE = 316, 512, 2560
HALF = TABLE // 2
UNROLL = 8
LANE_OFFSETS = (1, 4, 7)


def dot(a, b):
    return jnp.dot(a, b, preferred_element_type=F32)


def dot_t(a, b):
    return lax.dot_general(a, b, (((1,), (1,)), ((), ())), preferred_element_type=F32)


def lane_gather(block, index):
    numbers = lax.GatherDimensionNumbers(
        offset_dims=(),
        collapsed_slice_dims=(1,),
        start_index_map=(1,),
        operand_batching_dims=(0,),
        start_indices_batching_dims=(0,),
    )
    return lax.gather(
        block, index[..., None], numbers, (1, 1), mode=lax.GatherScatterMode.PROMISE_IN_BOUNDS
    )


def gather_by_lanes(row, table):
    columns = []
    for start in range(0, row.shape[1], 128):
        index = jnp.broadcast_to(row[:, start : start + 128], (16, 128))
        low = (index & 127).astype(jnp.int16)
        high = (index >> 7).astype(jnp.int16)
        parts = [jnp.zeros((16, 128), BF16)] * 4
        for block in range(table.shape[1] // 128):
            here = high == block
            for part in range(4):
                values = table[part * 16 : part * 16 + 16, block * 128 : block * 128 + 128]
                parts[part] = jnp.where(here, lane_gather(values, low), parts[part])
        columns.append(jnp.concatenate(parts, axis=0))
    return jnp.concatenate(columns, axis=1)


def gather_by_product(row, pieces, numbers):
    second = row >= HALF
    low = jnp.where(second, row - HALF, row)
    one, zero = jnp.ones((32, CELLS), F8), jnp.zeros((32, CELLS), F8)
    digit = jnp.broadcast_to((low & 255) - 128, (32, CELLS)).astype(jnp.int8)
    tile = jnp.broadcast_to(low >> 8, (32, CELLS)).astype(jnp.int8)
    chosen = [jnp.where(tile == at, one, zero) for at in range(HALF // 256)]
    equal = [digit == numbers[at * 32 : at * 32 + 32, :] for at in range(8)]
    hot = jnp.concatenate(
        [jnp.where(equal[at], value, zero) for value in chosen for at in range(8)], axis=0
    )
    out = dot(pieces, hot)
    second = jnp.broadcast_to(second, (64, CELLS))
    return (
        jnp.where(second, out[128:192], out[0:64]) + jnp.where(second, out[192:256], out[64:128])
    ).astype(BF16)


def children_of(count, child, width):
    rows = lax.broadcasted_iota(jnp.int32, (count, width), 0)
    columns = lax.broadcasted_iota(jnp.int32, (count, width), 1)
    return jnp.where(rows == 8 * columns + child, 1.0, 0.0).astype(BF16)


def upward(shifts_ref, level):
    total = None
    for child in range(8):
        part = dot(level, children_of(level.shape[1], child, 128)).astype(BF16)
        term = dot(shifts_ref[child], part)
        total = term if total is None else total + term
    return total


def exchange_kernel(
    leaf_ref, compress_ref, shifts_ref, boundary_ref,
    table_ref, parents_ref, top_ref,
    outgoing, incoming, term, terms, send, arrive, term_send, term_arrive,
):
    gx, gy = lax.axis_index("gx"), lax.axis_index("gy")

    def flipped(index, bit):
        step = 2**bit
        return index + step - 2 * step * ((index // step) % 2)

    partners = [(gx, flipped(gy, bit)) for bit in range(5)] + [
        (flipped(gx, bit), gy) for bit in range(3)
    ]
    octant = gy % 8
    peers = [(gx, gy - octant + (octant + apart) % 8) for apart in range(1, 8)]

    barrier = pltpu.get_barrier_semaphore()
    for device in partners + peers:
        pl.semaphore_signal(barrier, inc=1, device_id=device, device_id_type=MESH)

    packed = dot(compress_ref[...], leaf_ref[...]).astype(BF16)
    table_ref[:, 0:CELLS] = packed
    for section in range(8):
        outgoing[section] = gather_by_lanes(boundary_ref[section : section + 1, :], packed)

    pl.semaphore_wait(barrier, 15)
    copies = []
    for section in (4, 3, 1, 7, 2, 0, 6, 5):
        copy = pltpu.make_async_remote_copy(
            src_ref=outgoing.at[section],
            dst_ref=incoming.at[section],
            send_sem=send.at[section],
            recv_sem=arrive.at[section],
            device_id=partners[section],
            device_id_type=MESH,
        )
        copy.start()
        copies.append(copy)

    parents = upward(shifts_ref, leaf_ref[...]).astype(BF16)
    parents_ref[...] = parents
    grand = upward(shifts_ref, parents).astype(BF16)
    apex = upward(shifts_ref, grand)
    apex_row = apex.T[0:8, :].astype(BF16)
    own = dot_t(apex_row, shifts_ref[octant])
    term[...] = own
    term_copies = []
    for apart in range(1, 8):
        copy = pltpu.make_async_remote_copy(
            src_ref=term,
            dst_ref=terms.at[apart - 1],
            send_sem=term_send.at[apart - 1],
            recv_sem=term_arrive.at[apart - 1],
            device_id=peers[apart - 1],
            device_id_type=MESH,
        )
        copy.start()
        term_copies.append(copy)
    for copy in copies:
        copy.wait()
    for section in range(8):
        start = CELLS + section * 256
        table_ref[:, start : start + 256] = incoming[section]
    for copy in term_copies:
        copy.wait()
    total = own
    for apart in range(7):
        total = total + terms[apart]
    top_ref[...] = total


def far_kernel(
    table_ref, parents_ref, compress_ref, expand_ref, shifts_ref, transfer_ref, sources_ref, coarse_ref,
    out_ref,
    scaled, pieces, stack, total, coarse_stack, coarse_total, down,
):
    packed_parents = dot(compress_ref[...], parents_ref[...]).astype(BF16)
    coarse_total[...] = jnp.zeros_like(coarse_total)

    def coarse_group(step, carry):
        for pair in range(2):
            rows = [coarse_ref[pl.ds(step * 4 + pair * 2 + at, 1), :] for at in range(2)]
            index = jnp.broadcast_to(jnp.concatenate(rows, axis=1), (16, 128)).astype(jnp.int16)
            at = pl.multiple_of(step * 128 + pair * 64, 64)
            for part in range(4):
                coarse_stack[pl.ds(at + part * 16, 16), :] = lane_gather(
                    packed_parents[part * 16 : part * 16 + 16, :], index
                )
        return carry

    lax.fori_loop(0, OFFSETS // 4, coarse_group, 0, unroll=4)

    def coarse_product(step, carry):
        operators = [transfer_ref[step * 4 + at] for at in range(4)]
        left = jnp.concatenate(
            [
                jnp.concatenate([operators[0], operators[2]], axis=1),
                jnp.concatenate([operators[1], operators[3]], axis=1),
            ],
            axis=0,
        )
        at = pl.multiple_of(step * 128, 128)
        coarse_total[...] += dot(left, coarse_stack[pl.ds(at, 128), :])
        return carry

    lax.fori_loop(0, OFFSETS // 4, coarse_product, 0, unroll=4)
    both = coarse_total[...]
    far_parent = (0.5 * (both[0:64, 0:64] + both[64:128, 64:128])).T.astype(BF16)
    local_rows = dot_t(far_parent, expand_ref[...]).astype(BF16)
    for child in range(8):
        term = dot(local_rows, shifts_ref[child])
        for chunk in range(3):
            piece = term[:, chunk * 128 : chunk * 128 + 128]
            if piece.shape[1] < 128:
                piece = jnp.pad(piece, ((0, 0), (0, 128 - piece.shape[1])))
            down[chunk, pl.ds(child, 64, stride=8), :] = piece

    table = table_ref[...].astype(F32)
    largest = jnp.max(jnp.max(jnp.abs(table), axis=1, keepdims=True), axis=0, keepdims=True)
    scale = jnp.full((1, 1), 0.5, F32)
    for power in (64, 32, 16, 8, 4, 2, 1):
        grown = scale * 2.0**power
        scale = jnp.where(largest * grown <= 448.0, grown, scale)
    table = table * scale
    scaled[...] = table.astype(BF16)
    upper = table.astype(F8)
    lower = (table - upper.astype(F32)).astype(F8)
    for half in range(2):
        pieces[half * 128 : half * 128 + 64, :] = upper[:, half * HALF : half * HALF + HALF]
        pieces[half * 128 + 64 : half * 128 + 128, :] = lower[:, half * HALF : half * HALF + HALF]

    numbers = (lax.broadcasted_iota(jnp.int32, (256, CELLS), 0) - 128).astype(jnp.int8)
    total[...] = jnp.zeros_like(total)
    stack[...] = jnp.zeros_like(stack)
    steps = -(-OFFSETS // UNROLL)

    def product(step):
        for group in range(UNROLL // 4):
            first = step * UNROLL + group * 4
            left = jnp.concatenate(
                [transfer_ref[jnp.minimum(first + at, OFFSETS - 1)] for at in range(4)], axis=1
            )
            total[...] += dot(left, stack[group * 256 : group * 256 + 256, :])

    def body(step, carry):
        product(jnp.maximum(step - 1, 0))
        for at in range(UNROLL):
            offset = step * UNROLL + at
            row = sources_ref[pl.ds(jnp.minimum(offset, OFFSETS - 1), 1), :]
            row = jnp.where(offset < OFFSETS, row, TABLE)
            if at in LANE_OFFSETS:
                stack[at * 64 : at * 64 + 64, :] = gather_by_lanes(row, scaled)
            else:
                stack[at * 64 : at * 64 + 64, :] = gather_by_product(row, pieces[...], numbers)
        return carry

    lax.fori_loop(0, steps, body, 0)
    product(steps - 1)
    far_leaf = (total[...] / scale).astype(BF16)
    for chunk in range(3):
        rows = min(128, out_ref.shape[0] - chunk * 128)
        out_ref[chunk * 128 : chunk * 128 + rows, :] = (
            dot(expand_ref[chunk * 128 : chunk * 128 + rows, :], far_leaf)
            + down[chunk].T[0:rows, :]
        )


def call_far(table, parents, compress, expand, shifts, transfer, sources, coarse_sources):
    width = parents.shape[0]
    return pl.pallas_call(
        far_kernel,
        out_shape=jax.ShapeDtypeStruct((width, CELLS), F32),
        in_specs=[VMEM] * 8,
        out_specs=VMEM,
        scratch_shapes=[
            pltpu.VMEM((64, TABLE), BF16),
            pltpu.VMEM((256, HALF), F8),
            pltpu.VMEM((UNROLL * 64, CELLS), BF16),
            pltpu.VMEM((64, CELLS), F32),
            pltpu.VMEM((OFFSETS * 32, 128), BF16),
            pltpu.VMEM((128, 128), F32),
            pltpu.VMEM((3, CELLS, 128), F32),
        ],
        compiler_params=pltpu.CompilerParams(vmem_limit_bytes=40 << 20),
        name="far_field",
    )(table, parents, compress, expand, shifts, transfer, sources, coarse_sources)


def on_device(leaf_weights, compress, expand, transfer, shifts, boundary, sources, coarse_sources):
    width = leaf_weights.shape[1]
    table, parents, top = pl.pallas_call(
        exchange_kernel,
        out_shape=(
            jax.ShapeDtypeStruct((64, TABLE), BF16),
            jax.ShapeDtypeStruct((width, 128), BF16),
            jax.ShapeDtypeStruct((8, width), F32),
        ),
        in_specs=[VMEM] * 4,
        out_specs=(VMEM,) * 3,
        scratch_shapes=[
            pltpu.VMEM((8, 64, 256), BF16),
            pltpu.VMEM((8, 64, 256), BF16),
            pltpu.VMEM((8, width), F32),
            pltpu.VMEM((7, 8, width), F32),
            pltpu.SemaphoreType.DMA((8,)),
            pltpu.SemaphoreType.DMA((8,)),
            pltpu.SemaphoreType.DMA((7,)),
            pltpu.SemaphoreType.DMA((7,)),
        ],
        compiler_params=pltpu.CompilerParams(
            collective_id=0, has_side_effects=True, vmem_limit_bytes=24 << 20
        ),
        name="exchange",
    )(leaf_weights[0], compress, shifts, boundary[0])
    leaf_locals = call_far(
        table, parents, compress, expand, shifts, transfer, sources[0], coarse_sources[0]
    )
    return leaf_locals[None], top[0:1]


def solution(mesh):
    return jax.shard_map(
        on_device,
        mesh=mesh,
        in_specs=(
            P(("gx", "gy"), None, None),
            P(),
            P(),
            P(),
            P(),
            P(("gx", "gy"), None, None),
            P(("gx", "gy"), None, None),
            P(("gx", "gy"), None, None),
        ),
        out_specs=(P(("gx", "gy"), None, None), P(("gx", "gy"), None)),
        check_vma=False,
    )
```

```python
import jax
import jax.numpy as jnp
from jax import lax
from jax.experimental import pallas as pl
from jax.experimental.pallas import tpu as pltpu
from jax.sharding import PartitionSpec as P

F32, BF16, F8 = jnp.float32, jnp.bfloat16, jnp.float8_e4m3fn
MESH = pl.DeviceIdType.MESH
VMEM = pl.BlockSpec(memory_space=pltpu.VMEM)
OFFSETS, CELLS, TABLE = 316, 512, 2560
HALF = TABLE // 2
UNROLL = 16
LANE_OFFSETS = (0, 3, 6, 9, 12)


def dot(a, b):
    return jnp.dot(a, b, preferred_element_type=F32)


def dot_t(a, b):
    return lax.dot_general(a, b, (((1,), (1,)), ((), ())), preferred_element_type=F32)


def lane_gather(block, index):
    numbers = lax.GatherDimensionNumbers(
        offset_dims=(),
        collapsed_slice_dims=(1,),
        start_index_map=(1,),
        operand_batching_dims=(0,),
        start_indices_batching_dims=(0,),
    )
    return lax.gather(
        block, index[..., None], numbers, (1, 1), mode=lax.GatherScatterMode.PROMISE_IN_BOUNDS
    )


def gather_by_lanes(row, table):
    columns = []
    for start in range(0, row.shape[1], 128):
        index = jnp.broadcast_to(row[:, start : start + 128], (16, 128))
        low = (index & 127).astype(jnp.int16)
        high = (index >> 7).astype(jnp.int16)
        parts = [jnp.zeros((16, 128), BF16)] * 4
        for block in range(table.shape[1] // 128):
            here = high == block
            for part in range(4):
                values = table[part * 16 : part * 16 + 16, block * 128 : block * 128 + 128]
                parts[part] = jnp.where(here, lane_gather(values, low), parts[part])
        columns.append(jnp.concatenate(parts, axis=0))
    return jnp.concatenate(columns, axis=1)


def gather_by_product(row, pieces, numbers):
    second = row >= HALF
    low = jnp.where(second, row - HALF, row)
    one, zero = jnp.ones((32, CELLS), F8), jnp.zeros((32, CELLS), F8)
    digit = jnp.broadcast_to((low & 255) - 128, (32, CELLS)).astype(jnp.int8)
    tile = jnp.broadcast_to(low >> 8, (32, CELLS)).astype(jnp.int8)
    chosen = [jnp.where(tile == at, one, zero) for at in range(HALF // 256)]
    equal = [digit == numbers[at * 32 : at * 32 + 32, :] for at in range(8)]
    hot = jnp.concatenate(
        [jnp.where(equal[at], value, zero) for value in chosen for at in range(8)], axis=0
    )
    out = dot(pieces, hot)
    second = jnp.broadcast_to(second, (64, CELLS))
    return (
        jnp.where(second, out[128:192], out[0:64]) + jnp.where(second, out[192:256], out[64:128])
    ).astype(BF16)


def children_of(count, child, width):
    rows = lax.broadcasted_iota(jnp.int32, (count, width), 0)
    columns = lax.broadcasted_iota(jnp.int32, (count, width), 1)
    return jnp.where(rows == 8 * columns + child, 1.0, 0.0).astype(BF16)


def upward(shifts_ref, level):
    total = None
    for child in range(8):
        part = dot(level, children_of(level.shape[1], child, 128)).astype(BF16)
        term = dot(shifts_ref[child], part)
        total = term if total is None else total + term
    return total


def lay_out_operators(columns_ref, operators_ref):
    for start in range(0, OFFSETS, 128):
        count = min(128, OFFSETS - start)
        unit = jnp.where(
            lax.broadcasted_iota(jnp.int32, (count, count), 0)
            == lax.broadcasted_iota(jnp.int32, (count, count), 1),
            1.0,
            0.0,
        ).astype(BF16)
        for first in range(0, 32, 2):
            rows = [columns_ref[64 * a : 64 * a + 64, start : start + count]
                    for a in (first, first + 32, first + 1, first + 33)]
            turned = dot_t(unit, jnp.concatenate(rows, axis=0))
            for at in range(2):
                operators_ref[pl.ds(start * 32 + first + at, count, stride=32), :] = turned[
                    :, at * 128 : at * 128 + 128
                ]


def operators_of(operators_ref, offset):
    both = operators_ref[pl.ds(pl.multiple_of(offset * 32, 32), 32), :].astype(BF16)
    return both[:, 0:64], both[:, 64:128]


def exchange_kernel(
    leaf_ref, compress_ref, shifts_ref, boundary_ref, columns_ref,
    table_ref, parents_ref, top_ref, operators_ref,
    outgoing, incoming, term, terms, send, arrive, term_send, term_arrive,
):
    gx, gy = lax.axis_index("gx"), lax.axis_index("gy")

    def flipped(index, bit):
        step = 2**bit
        return index + step - 2 * step * ((index // step) % 2)

    partners = [(gx, flipped(gy, bit)) for bit in range(5)] + [
        (flipped(gx, bit), gy) for bit in range(3)
    ]
    octant = gy % 8
    peers = [(gx, gy - octant + (octant + apart) % 8) for apart in range(1, 8)]

    barrier = pltpu.get_barrier_semaphore()
    for device in partners + peers:
        pl.semaphore_signal(barrier, inc=1, device_id=device, device_id_type=MESH)

    packed = dot(compress_ref[...], leaf_ref[...]).astype(BF16)
    table_ref[:, 0:CELLS] = packed
    for section in range(8):
        outgoing[section] = gather_by_lanes(boundary_ref[section : section + 1, :], packed)

    pl.semaphore_wait(barrier, 15)
    copies = []
    for section in (4, 3, 1, 7, 2, 0, 6, 5):
        copy = pltpu.make_async_remote_copy(
            src_ref=outgoing.at[section],
            dst_ref=incoming.at[section],
            send_sem=send.at[section],
            recv_sem=arrive.at[section],
            device_id=partners[section],
            device_id_type=MESH,
        )
        copy.start()
        copies.append(copy)

    parents = upward(shifts_ref, leaf_ref[...]).astype(BF16)
    parents_ref[...] = parents
    grand = upward(shifts_ref, parents).astype(BF16)
    apex = upward(shifts_ref, grand)
    apex_row = apex.T[0:8, :].astype(BF16)
    own = dot_t(apex_row, shifts_ref[octant])
    term[...] = own
    term_copies = []
    for apart in range(1, 8):
        copy = pltpu.make_async_remote_copy(
            src_ref=term,
            dst_ref=terms.at[apart - 1],
            send_sem=term_send.at[apart - 1],
            recv_sem=term_arrive.at[apart - 1],
            device_id=peers[apart - 1],
            device_id_type=MESH,
        )
        copy.start()
        term_copies.append(copy)
    lay_out_operators(columns_ref, operators_ref)
    for copy in copies:
        copy.wait()
    for section in range(8):
        start = CELLS + section * 256
        table_ref[:, start : start + 256] = incoming[section]
    for copy in term_copies:
        copy.wait()
    total = own
    for apart in range(7):
        total = total + terms[apart]
    top_ref[...] = total[0:1, :]


def far_kernel(
    table_ref, parents_ref, compress_ref, expand_ref, shifts_ref, operators_ref, sources_ref, coarse_ref,
    out_ref,
    scaled, pieces, stack, total, coarse_rows, coarse_stack, coarse_total, down,
):
    packed_parents = dot(compress_ref[...], parents_ref[...]).astype(BF16)
    coarse_total[...] = jnp.zeros_like(coarse_total)
    coarse_rows[...] = coarse_ref[...].T

    table = table_ref[...].astype(F32)
    largest = jnp.max(jnp.max(jnp.abs(table), axis=1, keepdims=True), axis=0, keepdims=True)
    scale = jnp.full((1, 1), 0.5, F32)
    for power in (64, 32, 16, 8, 4, 2, 1):
        grown = scale * 2.0**power
        scale = jnp.where(largest * grown <= 448.0, grown, scale)
    table = table * scale
    scaled[...] = table.astype(BF16)
    upper = table.astype(F8)
    lower = (table - upper.astype(F32)).astype(F8)
    for half in range(2):
        pieces[half * 128 : half * 128 + 64, :] = upper[:, half * HALF : half * HALF + HALF]
        pieces[half * 128 + 64 : half * 128 + 128, :] = lower[:, half * HALF : half * HALF + HALF]

    numbers = (lax.broadcasted_iota(jnp.int32, (256, CELLS), 0) - 128).astype(jnp.int8)
    total[...] = jnp.zeros_like(total)
    stack[...] = jnp.zeros_like(stack)
    coarse_stack[...] = jnp.zeros_like(coarse_stack)
    steps = -(-OFFSETS // UNROLL)

    def product(step):
        for group in range(UNROLL // 4):
            first = step * UNROLL + group * 4
            operators = [
                operators_of(operators_ref, jnp.minimum(first + at, OFFSETS - 1)) for at in range(4)
            ]
            left = jnp.concatenate(
                [
                    jnp.concatenate([operators[at][half] for at in range(4)], axis=1)
                    for half in range(2)
                ],
                axis=0,
            )
            total[...] += dot(left, stack[group * 256 : group * 256 + 256, :])
            left = jnp.concatenate(
                [
                    jnp.concatenate([operators[at][half], operators[at + 2][half]], axis=1)
                    for at in range(2)
                    for half in range(2)
                ],
                axis=0,
            )
            coarse_total[...] += dot(left, coarse_stack[group * 128 : group * 128 + 128, :])

    def coarse_row(offset):
        row = coarse_rows[pl.ds(jnp.minimum(offset, OFFSETS - 1), 1), :]
        return jnp.where(offset < OFFSETS, row, 64)

    def body(step, carry):
        product(jnp.maximum(step - 1, 0))
        for pair in range(UNROLL // 2):
            rows = [coarse_row(step * UNROLL + pair * 2 + at) for at in range(2)]
            index = jnp.broadcast_to(jnp.concatenate(rows, axis=1), (16, 128)).astype(jnp.int16)
            for part in range(4):
                at = pair * 64 + part * 16
                coarse_stack[at : at + 16, :] = lane_gather(
                    packed_parents[part * 16 : part * 16 + 16, :], index
                )
        for at in range(UNROLL):
            offset = step * UNROLL + at
            row = sources_ref[jnp.minimum(offset, OFFSETS - 1)]
            row = jnp.where(offset < OFFSETS, row, TABLE)
            if at in LANE_OFFSETS:
                stack[at * 64 : at * 64 + 64, :] = gather_by_lanes(row, scaled)
            else:
                stack[at * 64 : at * 64 + 64, :] = gather_by_product(row, pieces[...], numbers)
        return carry

    lax.fori_loop(0, steps, body, 0)
    product(steps - 1)
    both = coarse_total[...]
    far_parent = (0.5 * (both[0:64, 0:64] + both[64:128, 64:128])).T.astype(BF16)
    local_rows = dot(far_parent, expand_ref[...]).astype(BF16)
    for child in range(8):
        term = dot(local_rows, shifts_ref[child])
        for chunk in range(3):
            piece = term[:, chunk * 128 : chunk * 128 + 128]
            if piece.shape[1] < 128:
                piece = jnp.pad(piece, ((0, 0), (0, 128 - piece.shape[1])))
            down[chunk, pl.ds(child, 64, stride=8), :] = piece

    far_leaf = (total[...] / scale).astype(BF16)
    expand = expand_ref[...].T
    for chunk in range(3):
        rows = min(128, out_ref.shape[0] - chunk * 128)
        out_ref[chunk * 128 : chunk * 128 + rows, :] = (
            dot(expand[chunk * 128 : chunk * 128 + rows, :], far_leaf)
            + down[chunk].T[0:rows, :]
        )


def call_far(table, parents, compress, expand, shifts, operators, sources, coarse_sources):
    width = parents.shape[0]
    return pl.pallas_call(
        far_kernel,
        out_shape=jax.ShapeDtypeStruct((width, CELLS), F32),
        in_specs=[VMEM] * 8,
        out_specs=VMEM,
        scratch_shapes=[
            pltpu.VMEM((64, TABLE), BF16),
            pltpu.VMEM((256, HALF), F8),
            pltpu.VMEM((UNROLL * 64, CELLS), BF16),
            pltpu.VMEM((64, CELLS), F32),
            pltpu.VMEM((OFFSETS, 64), jnp.int32),
            pltpu.VMEM((UNROLL * 32, 128), BF16),
            pltpu.VMEM((128, 128), F32),
            pltpu.VMEM((3, CELLS, 128), F32),
        ],
        compiler_params=pltpu.CompilerParams(vmem_limit_bytes=40 << 20),
        name="far_field",
    )(table, parents, compress, expand, shifts, operators, sources, coarse_sources)


def on_device(leaf_weights, compress, expand, transfer, shifts, boundary, sources, coarse_sources):
    width = leaf_weights.shape[1]
    columns = jnp.transpose(transfer, (1, 2, 0)).reshape(64 * 64, OFFSETS)
    table, parents, top, operators = pl.pallas_call(
        exchange_kernel,
        out_shape=(
            jax.ShapeDtypeStruct((64, TABLE), BF16),
            jax.ShapeDtypeStruct((width, 128), BF16),
            jax.ShapeDtypeStruct((1, width), F32),
            jax.ShapeDtypeStruct((OFFSETS * 32, 128), F32),
        ),
        in_specs=[VMEM] * 5,
        out_specs=(VMEM,) * 4,
        scratch_shapes=[
            pltpu.VMEM((8, 64, 256), BF16),
            pltpu.VMEM((8, 64, 256), BF16),
            pltpu.VMEM((8, width), F32),
            pltpu.VMEM((7, 8, width), F32),
            pltpu.SemaphoreType.DMA((8,)),
            pltpu.SemaphoreType.DMA((8,)),
            pltpu.SemaphoreType.DMA((7,)),
            pltpu.SemaphoreType.DMA((7,)),
        ],
        compiler_params=pltpu.CompilerParams(
            collective_id=0, has_side_effects=True, vmem_limit_bytes=24 << 20
        ),
        name="exchange",
    )(leaf_weights[0], compress, shifts, boundary[0], columns)
    leaf_locals = call_far(
        table,
        parents,
        compress,
        expand.T,
        shifts,
        operators,
        jnp.swapaxes(sources, 0, 1),
        coarse_sources[0].T,
    )
    return leaf_locals[None], top


def solution(mesh):
    return jax.shard_map(
        on_device,
        mesh=mesh,
        in_specs=(
            P(("gx", "gy"), None, None),
            P(),
            P(),
            P(),
            P(),
            P(("gx", "gy"), None, None),
            P(("gx", "gy"), None, None),
            P(("gx", "gy"), None, None),
        ),
        out_specs=(P(("gx", "gy"), None, None), P(("gx", "gy"), None)),
        check_vma=False,
    )
```

```python
import jax
import jax.numpy as jnp
from jax import lax
from jax.experimental import pallas as pl
from jax.experimental.pallas import tpu as pltpu
from jax.sharding import PartitionSpec as P

F32, BF16, F8 = jnp.float32, jnp.bfloat16, jnp.float8_e4m3fn
MESH = pl.DeviceIdType.MESH
VMEM = pl.BlockSpec(memory_space=pltpu.VMEM)
OFFSETS, CELLS, TABLE = 316, 512, 2560
HALF = TABLE // 2
UNROLL = 16
LANE_OFFSETS = (0, 3, 6, 9, 12)


def dot(a, b):
    return jnp.dot(a, b, preferred_element_type=F32)


def dot_t(a, b):
    return lax.dot_general(a, b, (((1,), (1,)), ((), ())), preferred_element_type=F32)


def repeat(rows, count):
    return jnp.concatenate([rows] * count, axis=0)


def lane_gather(block, index):
    numbers = lax.GatherDimensionNumbers(
        offset_dims=(),
        collapsed_slice_dims=(1,),
        start_index_map=(1,),
        operand_batching_dims=(0,),
        start_indices_batching_dims=(0,),
    )
    return lax.gather(
        block, index[..., None], numbers, (1, 1), mode=lax.GatherScatterMode.PROMISE_IN_BOUNDS
    )


def gather_by_lanes(row, table):
    columns = []
    for start in range(0, row.shape[1], 128):
        index = row[:, start : start + 128]
        low = repeat(index & 127, 2).astype(jnp.int16)
        high = repeat(index >> 7, 2).astype(jnp.int16)
        parts = [jnp.zeros((16, 128), BF16)] * 4
        for block in range(table.shape[1] // 128):
            here = high == block
            for part in range(4):
                values = table[part * 16 : part * 16 + 16, block * 128 : block * 128 + 128]
                parts[part] = jnp.where(here, lane_gather(values, low), parts[part])
        columns.append(jnp.concatenate(parts, axis=0))
    return jnp.concatenate(columns, axis=1)


def gather_by_product(row, pieces, numbers):
    second = row >= HALF
    low = jnp.where(second, row - HALF, row)
    one, zero = jnp.ones((32, CELLS), F8), jnp.zeros((32, CELLS), F8)
    digit = repeat((low & 255) - 128, 4).astype(jnp.int8)
    tile = repeat(low >> 8, 4).astype(jnp.int8)
    chosen = [jnp.where(tile == at, one, zero) for at in range(HALF // 256)]
    equal = [digit == numbers[at * 32 : at * 32 + 32, :] for at in range(8)]
    hot = jnp.concatenate(
        [jnp.where(equal[at], value, zero) for value in chosen for at in range(8)], axis=0
    )
    out = dot(pieces, hot)
    second = repeat(row, 8) >= HALF
    return (
        jnp.where(second, out[128:192], out[0:64]) + jnp.where(second, out[192:256], out[64:128])
    ).astype(BF16)


def children_of(count, child, width):
    rows = lax.broadcasted_iota(jnp.int32, (count, width), 0)
    columns = lax.broadcasted_iota(jnp.int32, (count, width), 1)
    return jnp.where(rows == 8 * columns + child, 1.0, 0.0).astype(BF16)


def upward(shifts_ref, level):
    total = None
    for child in range(8):
        part = dot(level, children_of(level.shape[1], child, 128)).astype(BF16)
        term = dot(shifts_ref[child], part)
        total = term if total is None else total + term
    return total


def lay_out_operators(columns_ref, operators_ref):
    for start in range(0, OFFSETS, 128):
        count = min(128, OFFSETS - start)
        unit = jnp.where(
            lax.broadcasted_iota(jnp.int32, (count, count), 0)
            == lax.broadcasted_iota(jnp.int32, (count, count), 1),
            1.0,
            0.0,
        ).astype(BF16)
        for first in range(0, 32, 2):
            rows = [columns_ref[64 * a : 64 * a + 64, start : start + count]
                    for a in (first, first + 32, first + 1, first + 33)]
            turned = dot_t(unit, jnp.concatenate(rows, axis=0))
            for at in range(2):
                operators_ref[pl.ds(start * 32 + first + at, count, stride=32), :] = turned[
                    :, at * 128 : at * 128 + 128
                ]


def operators_of(operators_ref, offset):
    both = operators_ref[pl.ds(pl.multiple_of(offset * 32, 32), 32), :].astype(BF16)
    return both[:, 0:64], both[:, 64:128]


def exchange_kernel(
    leaf_ref, compress_ref, shifts_ref, boundary_ref, columns_ref,
    table_ref, parents_ref, top_ref, operators_ref,
    outgoing, incoming, term, terms, send, arrive, term_send, term_arrive,
):
    gx, gy = lax.axis_index("gx"), lax.axis_index("gy")

    def flipped(index, bit):
        step = 2**bit
        return index + step - 2 * step * ((index // step) % 2)

    partners = [(gx, flipped(gy, bit)) for bit in range(5)] + [
        (flipped(gx, bit), gy) for bit in range(3)
    ]
    octant = gy % 8
    peers = [(gx, gy - octant + (octant + apart) % 8) for apart in range(1, 8)]

    barrier = pltpu.get_barrier_semaphore()
    for device in partners + peers:
        pl.semaphore_signal(barrier, inc=1, device_id=device, device_id_type=MESH)

    packed = dot(compress_ref[...], leaf_ref[...]).astype(BF16)
    table_ref[:, 0:CELLS] = packed
    for section in range(8):
        outgoing[section] = gather_by_lanes(
            jnp.broadcast_to(boundary_ref[section : section + 1, :], (8, 256)), packed
        )

    parents = upward(shifts_ref, leaf_ref[...]).astype(BF16)
    parents_ref[...] = parents
    grand = upward(shifts_ref, parents).astype(BF16)
    apex = upward(shifts_ref, grand)
    apex_row = apex.T[0:8, :].astype(BF16)
    own = dot_t(apex_row, shifts_ref[octant])
    term[...] = own
    pl.semaphore_wait(barrier, 15)
    copies = []
    for section in (4, 3, 1, 7, 2, 0, 6, 5):
        copy = pltpu.make_async_remote_copy(
            src_ref=outgoing.at[section],
            dst_ref=incoming.at[section],
            send_sem=send.at[section],
            recv_sem=arrive.at[section],
            device_id=partners[section],
            device_id_type=MESH,
        )
        copy.start()
        copies.append(copy)
    term_copies = []
    for apart in range(1, 8):
        copy = pltpu.make_async_remote_copy(
            src_ref=term,
            dst_ref=terms.at[apart - 1],
            send_sem=term_send.at[apart - 1],
            recv_sem=term_arrive.at[apart - 1],
            device_id=peers[apart - 1],
            device_id_type=MESH,
        )
        copy.start()
        term_copies.append(copy)
    lay_out_operators(columns_ref, operators_ref)
    for copy in copies:
        copy.wait()
    for section in range(8):
        start = CELLS + section * 256
        table_ref[:, start : start + 256] = incoming[section]
    for copy in term_copies:
        copy.wait()
    total = own
    for apart in range(7):
        total = total + terms[apart]
    top_ref[...] = total[0:1, :]


def far_kernel(
    table_ref, parents_ref, compress_ref, expand_ref, shifts_ref, operators_ref, sources_ref, coarse_ref, total_ref,
    out_ref, top_ref,
    scaled, pieces, stack, total, coarse_rows, coarse_stack, coarse_total, down,
):
    packed_parents = dot(compress_ref[...], parents_ref[...]).astype(BF16)
    coarse_total[...] = jnp.zeros_like(coarse_total)
    coarse_rows[...] = coarse_ref[...].T

    table = table_ref[...].astype(F32)
    largest = jnp.max(jnp.max(jnp.abs(table), axis=1, keepdims=True), axis=0, keepdims=True)
    scale = jnp.full((1, 1), 0.5, F32)
    for power in (64, 32, 16, 8, 4, 2, 1):
        grown = scale * 2.0**power
        scale = jnp.where(largest * grown <= 448.0, grown, scale)
    table = table * scale
    scaled[...] = table.astype(BF16)
    upper = table.astype(F8)
    lower = (table - upper.astype(F32)).astype(F8)
    for half in range(2):
        pieces[half * 128 : half * 128 + 64, :] = upper[:, half * HALF : half * HALF + HALF]
        pieces[half * 128 + 64 : half * 128 + 128, :] = lower[:, half * HALF : half * HALF + HALF]

    numbers = (lax.broadcasted_iota(jnp.int32, (256, CELLS), 0) - 128).astype(jnp.int8)
    total[...] = jnp.zeros_like(total)
    stack[...] = jnp.zeros_like(stack)
    coarse_stack[...] = jnp.zeros_like(coarse_stack)
    steps = -(-OFFSETS // UNROLL)

    def product(step):
        for group in range(UNROLL // 4):
            first = step * UNROLL + group * 4
            operators = [
                operators_of(operators_ref, jnp.minimum(first + at, OFFSETS - 1)) for at in range(4)
            ]
            left = jnp.concatenate(
                [
                    jnp.concatenate([operators[at][half] for at in range(4)], axis=1)
                    for half in range(2)
                ],
                axis=0,
            )
            total[...] += dot(left, stack[group * 256 : group * 256 + 256, :])
            left = jnp.concatenate(
                [
                    jnp.concatenate([operators[at][half], operators[at + 2][half]], axis=1)
                    for at in range(2)
                    for half in range(2)
                ],
                axis=0,
            )
            coarse_total[...] += dot(left, coarse_stack[group * 128 : group * 128 + 128, :])

    def coarse_row(offset):
        row = coarse_rows[pl.ds(jnp.minimum(offset, OFFSETS - 1), 1), :]
        return jnp.where(offset < OFFSETS, row, 64)

    def body(step, carry):
        product(jnp.maximum(step - 1, 0))
        for pair in range(UNROLL // 2):
            rows = [coarse_row(step * UNROLL + pair * 2 + at) for at in range(2)]
            index = jnp.broadcast_to(jnp.concatenate(rows, axis=1), (16, 128)).astype(jnp.int16)
            for part in range(4):
                at = pair * 64 + part * 16
                coarse_stack[at : at + 16, :] = lane_gather(
                    packed_parents[part * 16 : part * 16 + 16, :], index
                )
        for at in range(UNROLL):
            offset = step * UNROLL + at
            row = jnp.broadcast_to(sources_ref[jnp.minimum(offset, OFFSETS - 1)], (8, CELLS))
            row = jnp.where(offset < OFFSETS, row, TABLE)
            if at in LANE_OFFSETS:
                stack[at * 64 : at * 64 + 64, :] = gather_by_lanes(row, scaled)
            else:
                stack[at * 64 : at * 64 + 64, :] = gather_by_product(row, pieces[...], numbers)
        return carry

    lax.fori_loop(0, steps, body, 0)
    product(steps - 1)
    both = coarse_total[...]
    far_parent = (0.5 * (both[0:64, 0:64] + both[64:128, 64:128])).T.astype(BF16)
    local_rows = dot(far_parent, expand_ref[...]).astype(BF16)
    for child in range(8):
        term = dot(local_rows, shifts_ref[child])
        for chunk in range(3):
            piece = term[:, chunk * 128 : chunk * 128 + 128]
            if piece.shape[1] < 128:
                piece = jnp.pad(piece, ((0, 0), (0, 128 - piece.shape[1])))
            down[chunk, pl.ds(child, 64, stride=8), :] = piece

    far_leaf = (total[...] / scale).astype(BF16)
    top_ref[...] = total_ref[...]
    expand = expand_ref[...].T
    for chunk in range(3):
        rows = min(128, expand.shape[0] - chunk * 128)
        values = (
            dot(expand[chunk * 128 : chunk * 128 + rows, :], far_leaf)
            + down[chunk].T[0:rows, :]
        )
        for part in range(4):
            out_ref[pl.ds(chunk * 512 + part, rows, stride=4), :] = values[
                :, part * 128 : part * 128 + 128
            ]


def call_far(table, parents, compress, expand, shifts, operators, sources, coarse_sources, total):
    width = parents.shape[0]
    return pl.pallas_call(
        far_kernel,
        out_shape=(
            jax.ShapeDtypeStruct((width * 4, 128), F32),
            jax.ShapeDtypeStruct((1, width), F32),
        ),
        in_specs=[VMEM] * 9,
        out_specs=(VMEM,) * 2,
        scratch_shapes=[
            pltpu.VMEM((64, TABLE), BF16),
            pltpu.VMEM((256, HALF), F8),
            pltpu.VMEM((UNROLL * 64, CELLS), BF16),
            pltpu.VMEM((64, CELLS), F32),
            pltpu.VMEM((OFFSETS, 64), jnp.int32),
            pltpu.VMEM((UNROLL * 32, 128), BF16),
            pltpu.VMEM((128, 128), F32),
            pltpu.VMEM((3, CELLS, 128), F32),
        ],
        compiler_params=pltpu.CompilerParams(vmem_limit_bytes=40 << 20),
        name="far_field",
    )(table, parents, compress, expand, shifts, operators, sources, coarse_sources, total)


def on_device(leaf_weights, compress, expand, transfer, shifts, boundary, sources, coarse_sources):
    width = leaf_weights.shape[1]
    columns = jnp.transpose(transfer, (1, 2, 0)).reshape(64 * 64, OFFSETS)
    table, parents, top, operators = pl.pallas_call(
        exchange_kernel,
        out_shape=(
            jax.ShapeDtypeStruct((64, TABLE), BF16),
            jax.ShapeDtypeStruct((width, 128), BF16),
            jax.ShapeDtypeStruct((1, width), F32),
            jax.ShapeDtypeStruct((OFFSETS * 32, 128), F32),
        ),
        in_specs=[VMEM] * 5,
        out_specs=(VMEM,) * 4,
        scratch_shapes=[
            pltpu.VMEM((8, 64, 256), BF16),
            pltpu.VMEM((8, 64, 256), BF16),
            pltpu.VMEM((8, width), F32),
            pltpu.VMEM((7, 8, width), F32),
            pltpu.SemaphoreType.DMA((8,)),
            pltpu.SemaphoreType.DMA((8,)),
            pltpu.SemaphoreType.DMA((7,)),
            pltpu.SemaphoreType.DMA((7,)),
        ],
        compiler_params=pltpu.CompilerParams(
            collective_id=0, has_side_effects=True, vmem_limit_bytes=24 << 20
        ),
        name="exchange",
    )(leaf_weights[0], compress, shifts, boundary[0], columns)
    leaf_locals, top = call_far(
        table,
        parents,
        compress,
        expand.T,
        shifts,
        operators,
        jnp.swapaxes(sources, 0, 1),
        coarse_sources[0].T,
        top,
    )
    return leaf_locals.reshape(1, leaf_weights.shape[1], CELLS), top


def solution(mesh):
    return jax.shard_map(
        on_device,
        mesh=mesh,
        in_specs=(
            P(("gx", "gy"), None, None),
            P(),
            P(),
            P(),
            P(),
            P(("gx", "gy"), None, None),
            P(("gx", "gy"), None, None),
            P(("gx", "gy"), None, None),
        ),
        out_specs=(P(("gx", "gy"), None, None), P(("gx", "gy"), None)),
        check_vma=False,
    )
```

```python
import jax
import jax.numpy as jnp
from jax import lax
from jax.experimental import pallas as pl
from jax.experimental.pallas import tpu as pltpu
from jax.sharding import PartitionSpec as P

F32, BF16, F8 = jnp.float32, jnp.bfloat16, jnp.float8_e4m3fn
MESH = pl.DeviceIdType.MESH
VMEM = pl.BlockSpec(memory_space=pltpu.VMEM)
OFFSETS, CELLS, TABLE = 316, 512, 2560
HALF = TABLE // 2
UNROLL = 16
LANE_OFFSETS = (0, 3, 6, 9, 12)


def dot(a, b):
    return jnp.dot(a, b, preferred_element_type=F32)


def dot_t(a, b):
    return lax.dot_general(a, b, (((1,), (1,)), ((), ())), preferred_element_type=F32)


def repeat(rows, count):
    return jnp.concatenate([rows] * count, axis=0)


def lane_gather(block, index):
    numbers = lax.GatherDimensionNumbers(
        offset_dims=(),
        collapsed_slice_dims=(1,),
        start_index_map=(1,),
        operand_batching_dims=(0,),
        start_indices_batching_dims=(0,),
    )
    return lax.gather(
        block, index[..., None], numbers, (1, 1), mode=lax.GatherScatterMode.PROMISE_IN_BOUNDS
    )


def gather_by_lanes(row, table):
    columns = []
    for start in range(0, row.shape[1], 128):
        index = row[:, start : start + 128]
        low = repeat(index & 127, 2).astype(jnp.int16)
        high = repeat(index >> 7, 2).astype(jnp.int16)
        parts = [jnp.zeros((16, 128), BF16)] * 4
        for block in range(table.shape[1] // 128):
            here = high == block
            for part in range(4):
                values = table[part * 16 : part * 16 + 16, block * 128 : block * 128 + 128]
                parts[part] = jnp.where(here, lane_gather(values, low), parts[part])
        columns.append(jnp.concatenate(parts, axis=0))
    return jnp.concatenate(columns, axis=1)


def gather_by_product(row, pieces, numbers):
    second = row >= HALF
    low = jnp.where(second, row - HALF, row)
    one, zero = jnp.ones((32, CELLS), F8), jnp.zeros((32, CELLS), F8)
    digit = repeat((low & 255) - 128, 4).astype(jnp.int8)
    tile = repeat(low >> 8, 4).astype(jnp.int8)
    chosen = [jnp.where(tile == at, one, zero) for at in range(HALF // 256)]
    equal = [digit == numbers[at * 32 : at * 32 + 32, :] for at in range(8)]
    hot = jnp.concatenate(
        [jnp.where(equal[at], value, zero) for value in chosen for at in range(8)], axis=0
    )
    out = dot(pieces, hot)
    second = repeat(row, 8) >= HALF
    return (
        jnp.where(second, out[128:192], out[0:64]) + jnp.where(second, out[192:256], out[64:128])
    ).astype(BF16)


def children_of(count, child, width):
    rows = lax.broadcasted_iota(jnp.int32, (count, width), 0)
    columns = lax.broadcasted_iota(jnp.int32, (count, width), 1)
    return jnp.where(rows == 8 * columns + child, 1.0, 0.0).astype(BF16)


def upward(shifts_ref, level):
    total = None
    for child in range(8):
        part = dot(level, children_of(level.shape[1], child, 128)).astype(BF16)
        term = dot(shifts_ref[child], part)
        total = term if total is None else total + term
    return total


def lay_out_operators(columns_ref, operators_ref):
    for start in range(0, OFFSETS, 128):
        count = min(128, OFFSETS - start)
        unit = jnp.where(
            lax.broadcasted_iota(jnp.int32, (count, count), 0)
            == lax.broadcasted_iota(jnp.int32, (count, count), 1),
            1.0,
            0.0,
        ).astype(BF16)
        for first in range(0, 32, 2):
            rows = [columns_ref[64 * a : 64 * a + 64, start : start + count]
                    for a in (first, first + 32, first + 1, first + 33)]
            turned = dot_t(unit, jnp.concatenate(rows, axis=0))
            for at in range(2):
                operators_ref[pl.ds(start * 32 + first + at, count, stride=32), :] = turned[
                    :, at * 128 : at * 128 + 128
                ]


def operators_of(operators_ref, offset):
    both = operators_ref[pl.ds(pl.multiple_of(offset * 32, 32), 32), :].astype(BF16)
    return both[:, 0:64], both[:, 64:128]


def exchange_kernel(
    leaf_ref, compress_ref, shifts_ref, boundary_ref, columns_ref,
    table_ref, parents_ref, top_ref, operators_ref,
    outgoing, incoming, term, terms, send, arrive, term_send, term_arrive,
):
    gx, gy = lax.axis_index("gx"), lax.axis_index("gy")

    def flipped(index, bit):
        step = 2**bit
        return index + step - 2 * step * ((index // step) % 2)

    partners = [(gx, flipped(gy, bit)) for bit in range(5)] + [
        (flipped(gx, bit), gy) for bit in range(3)
    ]
    octant = gy % 8
    peers = [(gx, gy - octant + (octant + apart) % 8) for apart in range(1, 8)]

    barrier = pltpu.get_barrier_semaphore()
    for device in partners + peers:
        pl.semaphore_signal(barrier, inc=1, device_id=device, device_id_type=MESH)

    packed = dot(compress_ref[...], leaf_ref[...]).astype(BF16)
    table_ref[:, 0:CELLS] = packed
    for section in range(8):
        outgoing[section] = gather_by_lanes(
            jnp.broadcast_to(boundary_ref[section : section + 1, :], (8, 256)), packed
        )

    parents = upward(shifts_ref, leaf_ref[...]).astype(BF16)
    parents_ref[...] = parents
    grand = upward(shifts_ref, parents).astype(BF16)
    apex = upward(shifts_ref, grand)
    apex_row = apex.T[0:8, :].astype(BF16)
    own = dot_t(apex_row, shifts_ref[octant])
    term[...] = own
    pl.semaphore_wait(barrier, 15)
    copies = []
    for section in (4, 3, 1, 7, 2, 0, 6, 5):
        copy = pltpu.make_async_remote_copy(
            src_ref=outgoing.at[section],
            dst_ref=incoming.at[section],
            send_sem=send.at[section],
            recv_sem=arrive.at[section],
            device_id=partners[section],
            device_id_type=MESH,
        )
        copy.start()
        copies.append(copy)
    term_copies = []
    for apart in range(1, 8):
        copy = pltpu.make_async_remote_copy(
            src_ref=term,
            dst_ref=terms.at[apart - 1],
            send_sem=term_send.at[apart - 1],
            recv_sem=term_arrive.at[apart - 1],
            device_id=peers[apart - 1],
            device_id_type=MESH,
        )
        copy.start()
        term_copies.append(copy)
    lay_out_operators(columns_ref, operators_ref)
    for copy in copies:
        copy.wait()
    for section in range(8):
        start = CELLS + section * 256
        table_ref[:, start : start + 256] = incoming[section]
    for copy in term_copies:
        copy.wait()
    total = own
    for apart in range(7):
        total = total + terms[apart]
    top_ref[...] = total[0:1, :]


def far_kernel(
    table_ref, parents_ref, compress_ref, expand_ref, shifts_ref, operators_ref, sources_ref, coarse_ref, total_ref,
    out_ref, top_ref,
    scaled, pieces, stack, total, coarse_rows, coarse_stack, coarse_total, down,
):
    packed_parents = dot(compress_ref[...], parents_ref[...]).astype(BF16)
    coarse_total[...] = jnp.zeros_like(coarse_total)
    coarse_rows[...] = coarse_ref[...].T

    table = table_ref[...].astype(F32)
    largest = jnp.max(jnp.max(jnp.abs(table), axis=1, keepdims=True), axis=0, keepdims=True)
    scale = jnp.full((1, 1), 0.5, F32)
    for power in (64, 32, 16, 8, 4, 2, 1):
        grown = scale * 2.0**power
        scale = jnp.where(largest * grown <= 448.0, grown, scale)
    table = table * scale
    scaled[...] = table.astype(BF16)
    upper = table.astype(F8)
    lower = (table - upper.astype(F32)).astype(F8)
    for half in range(2):
        pieces[half * 128 : half * 128 + 64, :] = upper[:, half * HALF : half * HALF + HALF]
        pieces[half * 128 + 64 : half * 128 + 128, :] = lower[:, half * HALF : half * HALF + HALF]

    numbers = (lax.broadcasted_iota(jnp.int32, (256, CELLS), 0) - 128).astype(jnp.int8)
    total[...] = jnp.zeros_like(total)
    stack[...] = jnp.zeros_like(stack)
    coarse_stack[...] = jnp.zeros_like(coarse_stack)
    steps = -(-OFFSETS // UNROLL)

    def product(step):
        for group in range(UNROLL // 4):
            first = step * UNROLL + group * 4
            operators = [
                operators_of(operators_ref, jnp.minimum(first + at, OFFSETS - 1)) for at in range(4)
            ]
            left = jnp.concatenate(
                [
                    jnp.concatenate([operators[at][half] for at in range(4)], axis=1)
                    for half in range(2)
                ],
                axis=0,
            )
            total[...] += dot(left, stack[group * 256 : group * 256 + 256, :])
            left = jnp.concatenate(
                [
                    jnp.concatenate([operators[at][half], operators[at + 2][half]], axis=1)
                    for at in range(2)
                    for half in range(2)
                ],
                axis=0,
            )
            coarse_total[...] += dot(left, coarse_stack[group * 128 : group * 128 + 128, :])

    def coarse_row(offset):
        row = coarse_rows[pl.ds(jnp.minimum(offset, OFFSETS - 1), 1), :]
        return jnp.where(offset < OFFSETS, row, 64)

    def body(step, carry):
        product(jnp.maximum(step - 1, 0))
        for pair in range(UNROLL // 2):
            rows = [coarse_row(step * UNROLL + pair * 2 + at) for at in range(2)]
            index = jnp.broadcast_to(jnp.concatenate(rows, axis=1), (16, 128)).astype(jnp.int16)
            for part in range(4):
                at = pair * 64 + part * 16
                coarse_stack[at : at + 16, :] = lane_gather(
                    packed_parents[part * 16 : part * 16 + 16, :], index
                )
        for at in range(UNROLL):
            offset = step * UNROLL + at
            row = jnp.broadcast_to(sources_ref[jnp.minimum(offset, OFFSETS - 1)], (8, CELLS))
            row = jnp.where(offset < OFFSETS, row, TABLE)
            if at in LANE_OFFSETS:
                stack[at * 64 : at * 64 + 64, :] = gather_by_lanes(row, scaled)
            else:
                stack[at * 64 : at * 64 + 64, :] = gather_by_product(row, pieces[...], numbers)
        return carry

    lax.fori_loop(0, steps, body, 0)
    product(steps - 1)
    both = coarse_total[...]
    far_parent = (0.5 * (both[0:64, 0:64] + both[64:128, 64:128])).T.astype(BF16)
    local_rows = dot(far_parent, expand_ref[...]).astype(BF16)
    for child in range(8):
        term = dot(local_rows, shifts_ref[child])
        for chunk in range(3):
            piece = term[:, chunk * 128 : chunk * 128 + 128]
            if piece.shape[1] < 128:
                piece = jnp.pad(piece, ((0, 0), (0, 128 - piece.shape[1])))
            down[chunk, pl.ds(child, 64, stride=8), :] = piece

    far_leaf = (total[...] / scale).astype(BF16)
    top_ref[...] = total_ref[...]
    expand = expand_ref[...].T
    for chunk in range(3):
        rows = min(128, expand.shape[0] - chunk * 128)
        values = (
            dot(expand[chunk * 128 : chunk * 128 + rows, :], far_leaf)
            + down[chunk].T[0:rows, :]
        )
        for part in range(4):
            out_ref[chunk * 128 : chunk * 128 + rows, part, :] = values[
                :, part * 128 : part * 128 + 128
            ]


def call_far(table, parents, compress, expand, shifts, operators, sources, coarse_sources, total):
    width = parents.shape[0]
    return pl.pallas_call(
        far_kernel,
        out_shape=(
            jax.ShapeDtypeStruct((width, 4, 128), F32),
            jax.ShapeDtypeStruct((1, width), F32),
        ),
        in_specs=[VMEM] * 9,
        out_specs=(VMEM,) * 2,
        scratch_shapes=[
            pltpu.VMEM((64, TABLE), BF16),
            pltpu.VMEM((256, HALF), F8),
            pltpu.VMEM((UNROLL * 64, CELLS), BF16),
            pltpu.VMEM((64, CELLS), F32),
            pltpu.VMEM((OFFSETS, 64), jnp.int32),
            pltpu.VMEM((UNROLL * 32, 128), BF16),
            pltpu.VMEM((128, 128), F32),
            pltpu.VMEM((3, CELLS, 128), F32),
        ],
        compiler_params=pltpu.CompilerParams(vmem_limit_bytes=40 << 20),
        name="far_field",
    )(table, parents, compress, expand, shifts, operators, sources, coarse_sources, total)


def on_device(leaf_weights, compress, expand, transfer, shifts, boundary, sources, coarse_sources):
    width = leaf_weights.shape[1]
    columns = jnp.transpose(transfer, (1, 2, 0)).reshape(64 * 64, OFFSETS)
    table, parents, top, operators = pl.pallas_call(
        exchange_kernel,
        out_shape=(
            jax.ShapeDtypeStruct((64, TABLE), BF16),
            jax.ShapeDtypeStruct((width, 128), BF16),
            jax.ShapeDtypeStruct((1, width), F32),
            jax.ShapeDtypeStruct((OFFSETS * 32, 128), F32),
        ),
        in_specs=[VMEM] * 5,
        out_specs=(VMEM,) * 4,
        scratch_shapes=[
            pltpu.VMEM((8, 64, 256), BF16),
            pltpu.VMEM((8, 64, 256), BF16),
            pltpu.VMEM((8, width), F32),
            pltpu.VMEM((7, 8, width), F32),
            pltpu.SemaphoreType.DMA((8,)),
            pltpu.SemaphoreType.DMA((8,)),
            pltpu.SemaphoreType.DMA((7,)),
            pltpu.SemaphoreType.DMA((7,)),
        ],
        compiler_params=pltpu.CompilerParams(
            collective_id=0, has_side_effects=True, vmem_limit_bytes=24 << 20
        ),
        name="exchange",
    )(leaf_weights[0], compress, shifts, boundary[0], columns)
    leaf_locals, top = call_far(
        table,
        parents,
        compress,
        expand.T,
        shifts,
        operators,
        jnp.swapaxes(sources, 0, 1),
        coarse_sources[0].T,
        top,
    )
    return leaf_locals.reshape(1, leaf_weights.shape[1], CELLS), top


def solution(mesh):
    return jax.shard_map(
        on_device,
        mesh=mesh,
        in_specs=(
            P(("gx", "gy"), None, None),
            P(),
            P(),
            P(),
            P(),
            P(("gx", "gy"), None, None),
            P(("gx", "gy"), None, None),
            P(("gx", "gy"), None, None),
        ),
        out_specs=(P(("gx", "gy"), None, None), P(("gx", "gy"), None)),
        check_vma=False,
    )
```
